32 devices in a mesh: groups: 2 (over y), patch: 4 (over z), rows: 4 (over x, core).
Axes of the slice: x: 2, y: 2, z: 4, core: 2. Of those that a mesh axis runs over, the one named last changes fastest.
Arguments:
- panel: bfloat16 [2, 16384, 256], P(None, ('groups', 'patch', 'rows')), parts along dimension 1, may hold values from -6 to 6
- pairing: float32 [16384], P(('groups', 'patch', 'rows')), parts along dimension 0, may hold values from 0.1 to 0.5
- hop_blocks: bfloat16 [128, 8, 128, 128], P(('groups', 'patch', 'rows')), parts along dimension 0, may hold values from -0.09375 to 0.09375
- hop_cols: int32 [128, 8], P(('groups', 'patch', 'rows')), parts along dimension 0, may hold values from 0 to 15
- bnd_weight: bfloat16 [4096, 512], P(('groups', 'patch', 'rows')), parts along dimension 0, may hold values from -0.125 to 0.125
- attract: float32 [64], replicated, may hold values from 4 to 16
- attract_class: int32 [16384], P(('groups', 'patch', 'rows')), parts along dimension 0, may hold values from 0 to 63
- target: float32 [16384], P(('groups', 'patch', 'rows')), parts along dimension 0, may hold values from -6 to 6
Outputs:
- cheb_two: bfloat16 [2, 16384, 256], P(None, ('groups', 'patch', 'rows')), parts along dimension 1
- new_pair: float32 [16384], P(('groups', 'patch', 'rows')), parts along dimension 0
- class_grad: float32 [8, 64], P(('groups', 'patch'), 'rows'), parts along dimension 0
The draws below stay inside these ranges and needn't reach their ends.
There are 2 independent parts, one for each index of `groups`. The reference program is written for one: setup_inputs(seed, part) draws one part's arguments, and reference() takes and returns one part's arrays. A program takes and returns all parts, laid end to end along the dimension named above; an argument that names none is the same for every part. Nothing has to cross between parts.
Inputs may be any that keep to these rules, and one draw needn't show every extreme that they name: `hop_cols`: entries of a block row may repeat.
All inputs are finite; a program needn't handle non-finite values.
Results may differ from the reference program's by a relative error of at most 0.0044.
Values may be sent and summed in bfloat16 or wider, within the bound.
A program may use at most 64 MiB of HBM per device.

```python
import math
import jax
import jax.numpy as jnp
from jax import lax

ROWS_DEV = 512
COLS = 256
NB = 8
BND = 128
NPN = 4
NCLASS = 64
PATCH_SITES = 2048
SITES = 8192
HBLOCKS = 64
BROWS = 2048
N_PATCH = 4
N_ROWS = 4


def plant(drawn, stream_key, smallest, high):
    longest = drawn.shape.index(max(drawn.shape))
    spots = []
    for shift in (0, 1):
        where = [jax.random.randint(jax.random.fold_in(stream_key, axis), (), 0, length) for axis, length in enumerate(drawn.shape)]
        where[longest] = (where[longest] + shift) % drawn.shape[longest]
        spots.append(tuple(where))
    return drawn.at[spots[0]].set(smallest).at[spots[1]].set(high)


def levels(rng, dims, shards, smallest, largest):
    gain = 1.0
    for dim, shards_of in shards:
        draws = jax.random.uniform(jax.random.fold_in(jax.random.fold_in(rng, 6), dim), (shards_of,), jnp.float32, smallest / len(shards), largest / len(shards))
        gain = gain * jnp.repeat(jnp.exp(draws), dims[dim] // shards_of).reshape((-1,) + (1,) * (len(dims) - 1 - dim))
    return gain


def gaussian(rng, extent, scale, most, shards=(), kind=jnp.bfloat16):
    entries = jax.random.normal(rng, extent, jnp.float32) * scale
    if len(shards) > 0:
        entries = levels(rng, extent, shards, -0.22, 0.18) * entries
    return jnp.clip(entries, min=-most, max=most).astype(kind)


def setup_inputs(seed: int = 0, part: int = 0) -> dict:
    splits = jax.random.split(jax.random.key(seed), 9)
    part_keys = jax.random.split(jax.random.fold_in(splits[8], part), 9)
    panel = gaussian(part_keys[0], (2, SITES, COLS), 1.0, 6.0, ((1, 16),))
    pairing = jnp.clip(0.1 + 0.4 * jax.random.uniform(part_keys[1], (SITES,), jnp.float32) ** levels(part_keys[1], (SITES,), ((0, 16),), -0.2, 0.2), 0.1, 0.5)
    hop_blocks = gaussian(part_keys[2], (HBLOCKS, NB, 128, 128), (4 * NB * 128) ** -0.5, 0.09375, ((0, 16),))
    hop_cols = plant(jax.random.randint(part_keys[3], (HBLOCKS, NB), 0, PATCH_SITES // 128), jax.random.fold_in(part_keys[3], 1), 0, (PATCH_SITES // 128) - 1).astype(jnp.int32)
    bnd_weight = gaussian(part_keys[4], (BROWS, NPN * BND), (4 * NPN * BND) ** -0.5, 0.125, ((0, 16),))
    attract = jnp.clip(jnp.exp(jax.random.uniform(splits[5], (NCLASS,), jnp.float32, math.log(4.0), math.log(16.0))), 4.0, 16.0)
    attract_class = plant(jax.random.randint(part_keys[6], (SITES,), 0, NCLASS), jax.random.fold_in(part_keys[6], 1), 0, NCLASS - 1).astype(jnp.int32)
    target = gaussian(part_keys[7], (SITES,), 1.0, 6.0, ((0, 16),), jnp.float32)
    return dict(panel=panel, pairing=pairing, hop_blocks=hop_blocks, hop_cols=hop_cols, bnd_weight=bnd_weight, attract=attract, attract_class=attract_class, target=target)


coef_zero = 0.5
coef_one = 0.55
coef_two = -0.3


def neighbour_table():
    own = jnp.arange(N_PATCH, dtype=jnp.int32)[:, None]
    offsets = jnp.array([-1, 1, -2, 2], dtype=jnp.int32)[None, :]
    return ((own + offsets) % N_PATCH).astype(jnp.int32)


def hop_apply(panel, hop_blocks, hop_cols, bnd_weight):
    width = panel.shape[2]
    pblocks = N_ROWS * ROWS_DEV // 128
    grid = panel.reshape(2, N_PATCH, pblocks, 128, width)
    hops = hop_blocks.reshape(N_PATCH, pblocks, NB, 128, 128)
    links = hop_cols.reshape(N_PATCH, pblocks, NB)

    def one_patch(items):
        blocks, hop, link = items
        picked = jnp.take(blocks, link, axis=1)
        return jnp.einsum('bnrs,cbnsk->cbrk', hop.astype(jnp.float32), picked.astype(jnp.float32))

    inner = lax.map(one_patch, (jnp.moveaxis(grid, 1, 0), hops, links))
    inner = jnp.moveaxis(inner, 0, 1).reshape(2, N_PATCH, N_ROWS, ROWS_DEV, width)
    slabs = panel.reshape(2, N_PATCH, N_ROWS, ROWS_DEV, width)[:, :, :, :BND]
    near = jnp.take(slabs, neighbour_table(), axis=1)
    near = jnp.moveaxis(near, 2, 3).reshape(2, N_PATCH, N_ROWS, NPN * BND, width)
    weights = bnd_weight.reshape(N_PATCH, N_ROWS, BND, NPN * BND)
    edge = jnp.einsum('prij,cprjk->cprik', weights.astype(jnp.float32), near.astype(jnp.float32))
    inner = inner.at[:, :, :, :BND].add(edge)
    return inner.reshape(2, SITES, width)


def bdg_apply(panel, pairing, hop_blocks, hop_cols, bnd_weight):
    hopped = hop_apply(panel, hop_blocks, hop_cols, bnd_weight)
    values = panel.astype(jnp.float32)
    particle = hopped[0] + pairing[:, None] * values[1]
    hole = pairing[:, None] * values[0] - hopped[1]
    return jnp.stack([particle, hole])


def reference(panel, pairing, hop_blocks, hop_cols, bnd_weight, attract, attract_class, target):
    first = bdg_apply(panel, pairing, hop_blocks, hop_cols, bnd_weight).astype(jnp.bfloat16)
    second = 2.0 * bdg_apply(first, pairing, hop_blocks, hop_cols, bnd_weight) - panel.astype(jnp.float32)
    cheb_two = second.astype(jnp.bfloat16)
    values = panel.astype(jnp.float32)
    moment = coef_zero * values[0] + coef_one * first[0].astype(jnp.float32) + coef_two * second[0]
    gvalue = jnp.sum(values[1] * moment, axis=1) / COLS
    new_pair = attract[attract_class] * gvalue
    patch_ids = jnp.arange(SITES, dtype=jnp.int32) // PATCH_SITES
    segment_ids = patch_ids * NCLASS + attract_class
    class_grad = jax.ops.segment_sum(target * gvalue, segment_ids, N_PATCH * NCLASS).reshape(N_PATCH, NCLASS)
    return cheb_two, new_pair, class_grad
```

```python
import functools

import jax
import jax.numpy as jnp
from jax import lax
from jax.experimental import pallas as pl
from jax.experimental.pallas import tpu as pltpu
from jax.sharding import PartitionSpec as P

coef_zero = 0.5
coef_one = 0.55
coef_two = -0.3

LANES = 128
BLOCK = 128
OFFSETS = (-1, 1, -2, 2)
MESH = pl.DeviceIdType.MESH
HIGHEST = lax.Precision.HIGHEST
LANE_DIMS = (((1,), (1,)), ((), ()))


def distinct(n_patch):
    shifts = []
    for offset in OFFSETS:
        if offset % n_patch not in shifts:
            shifts.append(offset % n_patch)
    return shifts


def kernel(
    n_rows, n_patch,
    cols_ref, pairing_ref, bnd_ref, attract_ref, class_ref, target_ref, panel_ref, hop_ref,
    cheb_ref, pair_out_ref, grad_ref,
    pbufs, fbufs, pnear, fnear, outs, hop, pair, moments, terms,
    peer_send, peer_recv, mate_send, mate_recv, fwd_send, fwd_recv,
    near_send, near_recv, term_send, term_recv, load_sem, hop_sem, store_sem,
):
    n_blocks = panel_ref.shape[1]
    rows = n_blocks * BLOCK
    width = panel_ref.shape[3]
    edge = bnd_ref.shape[0]
    edge_blocks = edge // BLOCK
    classes = attract_ref.shape[1]
    n_links = hop_ref.shape[1]
    halves = width // LANES
    shifts = distinct(n_patch)
    chunks = [(c, k) for c in range(2) for k in range(halves)]
    n_chunks = len(chunks)
    n_peers = n_rows // 2 - 1

    me = lax.axis_index("rows")
    patch = lax.axis_index("patch")
    mate = me + 1 - 2 * lax.rem(me, 2)

    def row_id(distance):
        return lax.rem(me + distance, n_rows)

    def span(owner):
        return pl.ds(owner * n_blocks, n_blocks)

    def patch_id(shift):
        return lax.rem(patch + shift, n_patch)

    barrier = pltpu.get_barrier_semaphore()
    for distance in range(1, n_rows):
        pl.semaphore_signal(barrier, inc=1, device_id={"rows": row_id(distance)}, device_id_type=MESH)
    for shift in shifts:
        pl.semaphore_signal(barrier, inc=1, device_id={"patch": patch_id(shift)}, device_id_type=MESH)

    hop_copy = pltpu.make_async_copy(hop_ref, hop, hop_sem)
    loads = []
    for i, (c, k) in enumerate(chunks):
        lanes = pl.ds(k * LANES, LANES)
        loads.append(
            pltpu.make_async_copy(panel_ref.at[c, :, :, lanes], pbufs[i].at[span(me)], load_sem.at[i])
        )
        loads[i].start()
    hop_copy.start()
    pl.semaphore_wait(barrier, n_rows - 1 + len(shifts))

    def sends(step, own, slab, dest, near):
        peers = [
            pltpu.make_async_remote_copy(
                own, dest.at[span(me)], peer_send.at[step, j], peer_recv.at[step, j],
                device_id={"rows": row_id(n_rows - 2 * (j + 1))}, device_id_type=MESH,
            )
            for j in range(n_peers)
        ]
        to_mate = pltpu.make_async_remote_copy(
            own, dest.at[span(me)], mate_send.at[step], mate_recv.at[step],
            device_id={"rows": mate}, device_id_type=MESH,
        )
        to_near = [
            pltpu.make_async_remote_copy(
                slab, near.at[pl.ds(j * edge_blocks, edge_blocks)], near_send.at[step, j], near_recv.at[step, j],
                device_id={"patch": patch_id(n_patch - shift)}, device_id_type=MESH,
            )
            for j, shift in enumerate(shifts)
        ]
        forwards = []
        for j in range(n_peers):
            block = dest.at[span(row_id(2 * (j + 1)))]
            forwards.append(
                pltpu.make_async_remote_copy(
                    block, block, fwd_send.at[step, j], fwd_recv.at[step, j],
                    device_id={"rows": mate}, device_id_type=MESH,
                )
            )
        return peers, to_mate, to_near, forwards

    def launch(copies):
        peers, to_mate, to_near, _ = copies
        for copy in peers + to_near + [to_mate]:
            copy.start()

    def arrive(copies):
        peers, to_mate, to_near, forwards = copies
        for peer, forward in zip(peers, forwards):
            peer.wait_recv()
            forward.start()
        to_mate.wait_recv()
        for copy in to_near:
            copy.wait_recv()
        for forward in forwards:
            forward.wait_recv()

    def hopped(buf, near, b):
        left = [hop[b, n] for n in range(n_links)]
        right = [buf[cols_ref[b, n]] for n in range(n_links)]
        if b * BLOCK < edge:
            left.append(bnd_ref[pl.ds(b * BLOCK, BLOCK), :])
            for offset in OFFSETS:
                slot = shifts.index(offset % n_patch) * edge_blocks
                right.extend(near[slot + e] for e in range(edge_blocks))
        return jnp.dot(
            jnp.concatenate(left, axis=1),
            jnp.concatenate(right, axis=0),
            preferred_element_type=jnp.float32,
        )

    started = []
    for i, (c, k) in enumerate(chunks):
        lanes = pl.ds(k * LANES, LANES)
        started.append(
            sends(i, panel_ref.at[c, :, :, lanes], panel_ref.at[c, pl.ds(0, edge_blocks), :, lanes], pbufs[i], pnear[i])
        )
        launch(started[i])

    for b in range(rows // BLOCK):
        sites = pl.ds(b * BLOCK, BLOCK)
        wide = jnp.broadcast_to(pairing_ref[:, sites], (BLOCK, BLOCK))
        pair[sites, :] = wide.T

    hop_copy.wait()
    for i in range(n_chunks):
        loads[i].wait()

    for i, (c, k) in enumerate(chunks):
        arrive(started[i])
        other = (1 - c) * halves + k
        for b in range(rows // BLOCK):
            sites = pl.ds(b * BLOCK, BLOCK)
            hv = hopped(pbufs[i], pnear[i], b)
            cross = pair[sites, :] * pbufs[other][me * n_blocks + b].astype(jnp.float32)
            value = cross + hv if c == 0 else cross - hv
            fbufs[i][me * n_blocks + b] = value.astype(jnp.bfloat16)
        started.append(
            sends(
                n_chunks + i, fbufs[i].at[span(me)],
                fbufs[i].at[pl.ds(me * n_blocks, edge_blocks)], fbufs[i], fnear[i],
            )
        )
        launch(started[n_chunks + i])

    term_copies = [
        pltpu.make_async_remote_copy(
            terms.at[0], terms.at[d], term_send.at[d - 1], term_recv.at[d - 1],
            device_id={"rows": row_id(n_rows - d)}, device_id_type=MESH,
        )
        for d in range(1, n_rows)
    ]
    stores = []
    for i, (c, k) in enumerate(chunks):
        arrive(started[n_chunks + i])
        other = (1 - c) * halves + k
        for b in range(rows // BLOCK):
            sites = pl.ds(b * BLOCK, BLOCK)
            mine = me * n_blocks + b
            hv = hopped(fbufs[i], fnear[i], b)
            cross = pair[sites, :] * fbufs[other][mine].astype(jnp.float32)
            before = pbufs[i][mine].astype(jnp.float32)
            second = 2.0 * (cross + hv if c == 0 else cross - hv) - before
            outs[i][b] = second.astype(jnp.bfloat16)
            if c == 0:
                moment = (
                    coef_zero * before
                    + coef_one * fbufs[i][mine].astype(jnp.float32)
                    + coef_two * second
                )
                weighted = pbufs[other][mine].astype(jnp.float32) * moment
                if k == 0:
                    moments[sites, :] = weighted
                else:
                    moments[sites, :] += weighted
        stores.append(
            pltpu.make_async_copy(
                outs[i], cheb_ref.at[c, :, :, pl.ds(k * LANES, LANES)], store_sem.at[i]
            )
        )
        stores[i].start()
        if c == 0 and k == halves - 1:
            ones = jnp.ones((8, LANES), jnp.float32)
            gvalue = lax.dot_general(
                ones, moments[...], LANE_DIMS, precision=HIGHEST,
                preferred_element_type=jnp.float32,
            ) / width
            numbers = lax.broadcasted_iota(jnp.int32, (classes, rows), 0)
            onehot = (numbers == class_ref[...]).astype(jnp.float32)
            gain = jnp.dot(
                jnp.broadcast_to(attract_ref[...], (8, classes)), onehot, precision=HIGHEST,
                preferred_element_type=jnp.float32,
            )
            pair_out_ref[...] = (gain * gvalue)[:1]
            terms[0] = lax.dot_general(
                target_ref[...] * gvalue, onehot, LANE_DIMS, precision=HIGHEST,
                preferred_element_type=jnp.float32,
            )
            for copy in term_copies:
                copy.start()

    for copy in term_copies:
        copy.wait_recv()
    total = terms[0]
    for d in range(1, n_rows):
        total = total + terms[d]
    share = classes // n_rows
    pick = (
        lax.broadcasted_iota(jnp.int32, (classes, share), 0)
        == lax.broadcasted_iota(jnp.int32, (classes, share), 1) + me * share
    ).astype(jnp.float32)
    grad_ref[...] = jnp.dot(
        total, pick, precision=HIGHEST, preferred_element_type=jnp.float32
    )[:1]

    for peers, to_mate, to_near, forwards in started:
        for copy in peers + [to_mate] + to_near + forwards:
            copy.wait_send()
    for copy in term_copies:
        copy.wait_send()
    for copy in stores:
        copy.wait()


def on_device(n_rows, n_patch, panel, pairing, hop_blocks, hop_cols, bnd_weight, attract, attract_class, target):
    _, rows, width = panel.shape
    edge = bnd_weight.shape[0]
    classes = attract.shape[0]
    n_chunks = 2 * (width // LANES)
    n_near = len(distinct(n_patch))
    n_peers = n_rows // 2 - 1
    dma = pltpu.SemaphoreType.DMA
    vmem = pl.BlockSpec(memory_space=pltpu.VMEM)
    anywhere = pl.BlockSpec(memory_space=pl.ANY)

    blocks = rows // BLOCK

    def each(count):
        return [pltpu.VMEM((count, BLOCK, LANES), jnp.bfloat16) for _ in range(n_chunks)]

    cheb_two, new_pair, class_grad = pl.pallas_call(
        functools.partial(kernel, n_rows, n_patch),
        out_shape=(
            jax.ShapeDtypeStruct((2, blocks, BLOCK, width), jnp.bfloat16),
            jax.ShapeDtypeStruct((1, rows), jnp.float32),
            jax.ShapeDtypeStruct((1, classes // n_rows), jnp.float32),
        ),
        in_specs=[pl.BlockSpec(memory_space=pltpu.SMEM)] + [vmem] * 5 + [anywhere] * 2,
        out_specs=(anywhere, vmem, vmem),
        scratch_shapes=[
            each(n_rows * blocks),
            each(n_rows * blocks),
            each(n_near * edge // BLOCK),
            each(n_near * edge // BLOCK),
            each(blocks),
            pltpu.VMEM(hop_blocks.shape, jnp.bfloat16),
            pltpu.VMEM((rows, LANES), jnp.float32),
            pltpu.VMEM((rows, LANES), jnp.float32),
            pltpu.VMEM((n_rows, 8, classes), jnp.float32),
            dma((2 * n_chunks, n_peers)),
            dma((2 * n_chunks, n_peers)),
            dma((2 * n_chunks,)),
            dma((2 * n_chunks,)),
            dma((2 * n_chunks, n_peers)),
            dma((2 * n_chunks, n_peers)),
            dma((2 * n_chunks, n_near)),
            dma((2 * n_chunks, n_near)),
            dma((n_rows - 1,)),
            dma((n_rows - 1,)),
            dma((n_chunks,)),
            dma,
            dma((n_chunks,)),
        ],
        compiler_params=pltpu.CompilerParams(
            collective_id=0, has_side_effects=True, vmem_limit_bytes=56 * 1024 * 1024
        ),
    )(
        hop_cols, pairing.reshape(1, rows), bnd_weight, attract.reshape(1, classes),
        attract_class.reshape(1, rows), target.reshape(1, rows),
        panel.reshape(2, blocks, BLOCK, width), hop_blocks,
    )
    return cheb_two.reshape(panel.shape), new_pair.reshape(rows), class_grad


def solution(mesh):
    return jax.shard_map(
        functools.partial(on_device, mesh.shape["rows"], mesh.shape["patch"]),
        mesh=mesh,
        in_specs=(
            P(None, ("groups", "patch", "rows"), None),
            P(("groups", "patch", "rows")),
            P(("groups", "patch", "rows"), None, None, None),
            P(("groups", "patch", "rows"), None),
            P(("groups", "patch", "rows"), None),
            P(),
            P(("groups", "patch", "rows")),
            P(("groups", "patch", "rows")),
        ),
        out_specs=(
            P(None, ("groups", "patch", "rows"), None),
            P(("groups", "patch", "rows")),
            P(("groups", "patch"), "rows"),
        ),
        check_vma=False,
    )
```

```python
import functools

import jax
import jax.numpy as jnp
from jax import lax
from jax.experimental import pallas as pl
from jax.experimental.pallas import tpu as pltpu
from jax.sharding import PartitionSpec as P

coef_zero = 0.5
coef_one = 0.55
coef_two = -0.3

LANES = 128
BLOCK = 128
OFFSETS = (-1, 1, -2, 2)
MESH = pl.DeviceIdType.MESH
HIGHEST = lax.Precision.HIGHEST
LANE_DIMS = (((1,), (1,)), ((), ()))


def distinct(n_patch):
    shifts = []
    for offset in OFFSETS:
        if offset % n_patch not in shifts:
            shifts.append(offset % n_patch)
    return shifts


def kernel(
    n_rows, n_patch,
    cols_ref, pairing_ref, bnd_hbm, attract_ref, class_ref, target_ref, panel_ref, hop_ref,
    cheb_ref, pair_out_ref, grad_ref,
    pbufs, fbufs, pnear, fnear, hop, pair, moments, terms,
    peer_send, peer_recv, mate_send, mate_recv, fwd_send, fwd_recv,
    near_send, near_recv, term_send, term_recv, load_sem, hop_sem, bnd_ref, bnd_sem,
):
    n_blocks = panel_ref.shape[1]
    rows = n_blocks * BLOCK
    width = panel_ref.shape[3]
    edge = bnd_ref.shape[0]
    edge_blocks = edge // BLOCK
    classes = attract_ref.shape[1]
    n_links = hop_ref.shape[1]
    halves = width // LANES
    shifts = distinct(n_patch)
    chunks = [(c, k) for c in range(2) for k in range(halves)]
    n_chunks = len(chunks)
    n_peers = n_rows // 2 - 1

    me = lax.axis_index("rows")
    patch = lax.axis_index("patch")
    mate = me + 1 - 2 * lax.rem(me, 2)

    def row_id(distance):
        return lax.rem(me + distance, n_rows)

    def span(owner):
        return pl.ds(owner * n_blocks, n_blocks)

    def patch_id(shift):
        return lax.rem(patch + shift, n_patch)

    barrier = pltpu.get_barrier_semaphore()
    for shift in reversed(shifts):
        pl.semaphore_signal(barrier, inc=1, device_id={"patch": patch_id(shift)}, device_id_type=MESH)
    for distance in range(1, n_rows):
        pl.semaphore_signal(barrier, inc=1, device_id={"rows": row_id(distance)}, device_id_type=MESH)

    bnd_copy = pltpu.make_async_copy(bnd_hbm, bnd_ref, bnd_sem)
    hop_copy = pltpu.make_async_copy(hop_ref, hop, hop_sem)
    loads = []
    for i, (c, k) in enumerate(chunks):
        lanes = pl.ds(k * LANES, LANES)
        loads.append(
            pltpu.make_async_copy(panel_ref.at[c, :, :, lanes], pbufs[i].at[span(me)], load_sem.at[i])
        )
        loads[i].start()
    hop_copy.start()
    bnd_copy.start()
    pl.semaphore_wait(barrier, n_rows - 1 + len(shifts))

    def sends(step, own, slab, dest, near):
        peers = [
            pltpu.make_async_remote_copy(
                own, dest.at[span(me)], peer_send.at[step, j], peer_recv.at[step, j],
                device_id={"rows": row_id(n_rows - 2 * (j + 1))}, device_id_type=MESH,
            )
            for j in range(n_peers)
        ]
        to_mate = pltpu.make_async_remote_copy(
            own, dest.at[span(me)], mate_send.at[step], mate_recv.at[step],
            device_id={"rows": mate}, device_id_type=MESH,
        )
        to_near = [
            pltpu.make_async_remote_copy(
                slab, near.at[pl.ds(j * edge_blocks, edge_blocks)], near_send.at[step, j], near_recv.at[step, j],
                device_id={"patch": patch_id(n_patch - shift)}, device_id_type=MESH,
            )
            for j, shift in enumerate(shifts)
        ]
        forwards = []
        for j in range(n_peers):
            block = dest.at[span(row_id(2 * (j + 1)))]
            forwards.append(
                pltpu.make_async_remote_copy(
                    block, block, fwd_send.at[step, j], fwd_recv.at[step, j],
                    device_id={"rows": mate}, device_id_type=MESH,
                )
            )
        return peers, to_mate, to_near, forwards

    def launch(copies):
        peers, to_mate, to_near, _ = copies
        for copy in peers + to_near + [to_mate]:
            copy.start()

    def arrive(copies):
        peers, to_mate, to_near, forwards = copies
        for peer, forward in zip(peers, forwards):
            peer.wait_recv()
            forward.start()
        to_mate.wait_recv()
        for copy in to_near:
            copy.wait_recv()
        for forward in forwards:
            forward.wait_recv()

    def hopped(buf, near, b):
        left = [hop[b, n] for n in range(n_links)]
        right = [buf[cols_ref[b, n]] for n in range(n_links)]
        if b * BLOCK < edge:
            left.append(bnd_ref[pl.ds(b * BLOCK, BLOCK), :])
            for offset in OFFSETS:
                slot = shifts.index(offset % n_patch) * edge_blocks
                right.extend(near[slot + e] for e in range(edge_blocks))
        return jnp.dot(
            jnp.concatenate(left, axis=1),
            jnp.concatenate(right, axis=0),
            preferred_element_type=jnp.float32,
        )

    started = []
    for i, (c, k) in enumerate(chunks):
        lanes = pl.ds(k * LANES, LANES)
        started.append(
            sends(i, panel_ref.at[c, :, :, lanes], panel_ref.at[c, pl.ds(0, edge_blocks), :, lanes], pbufs[i], pnear[i])
        )
        launch(started[i])

    for b in range(rows // BLOCK):
        sites = pl.ds(b * BLOCK, BLOCK)
        wide = jnp.broadcast_to(pairing_ref[:, sites], (BLOCK, BLOCK))
        pair[sites, :] = wide.T

    hop_copy.wait()
    bnd_copy.wait()
    for i in range(n_chunks):
        loads[i].wait()

    for i, (c, k) in enumerate(chunks):
        arrive(started[i])
        other = (1 - c) * halves + k
        for b in range(rows // BLOCK):
            sites = pl.ds(b * BLOCK, BLOCK)
            hv = hopped(pbufs[i], pnear[i], b)
            cross = pair[sites, :] * pbufs[other][me * n_blocks + b].astype(jnp.float32)
            value = cross + hv if c == 0 else cross - hv
            fbufs[i][me * n_blocks + b] = value.astype(jnp.bfloat16)
        started.append(
            sends(
                n_chunks + i, fbufs[i].at[span(me)],
                fbufs[i].at[pl.ds(me * n_blocks, edge_blocks)], fbufs[i], fnear[i],
            )
        )
        launch(started[n_chunks + i])

    term_copies = [
        pltpu.make_async_remote_copy(
            terms.at[0], terms.at[d], term_send.at[d - 1], term_recv.at[d - 1],
            device_id={"rows": row_id(n_rows - d)}, device_id_type=MESH,
        )
        for d in range(1, n_rows)
    ]
    for i, (c, k) in enumerate(chunks):
        arrive(started[n_chunks + i])
        other = (1 - c) * halves + k
        for b in range(rows // BLOCK):
            sites = pl.ds(b * BLOCK, BLOCK)
            mine = me * n_blocks + b
            hv = hopped(fbufs[i], fnear[i], b)
            cross = pair[sites, :] * fbufs[other][mine].astype(jnp.float32)
            before = pbufs[i][mine].astype(jnp.float32)
            second = 2.0 * (cross + hv if c == 0 else cross - hv) - before
            cheb_ref[c, b, :, pl.ds(k * LANES, LANES)] = second.astype(jnp.bfloat16)
            if c == 0:
                moment = (
                    coef_zero * before
                    + coef_one * fbufs[i][mine].astype(jnp.float32)
                    + coef_two * second
                )
                weighted = pbufs[other][mine].astype(jnp.float32) * moment
                if k == 0:
                    moments[sites, :] = weighted
                else:
                    moments[sites, :] += weighted
        if c == 0 and k == halves - 1:
            ones = jnp.ones((8, LANES), jnp.float32)
            gvalue = lax.dot_general(
                ones, moments[...], LANE_DIMS, precision=HIGHEST,
                preferred_element_type=jnp.float32,
            ) / width
            numbers = lax.broadcasted_iota(jnp.int32, (classes, rows), 0)
            onehot = (numbers == class_ref[...]).astype(jnp.float32)
            gain = jnp.dot(
                jnp.broadcast_to(attract_ref[...], (8, classes)), onehot, precision=HIGHEST,
                preferred_element_type=jnp.float32,
            )
            pair_out_ref[...] = (gain * gvalue)[:1]
            terms[0] = lax.dot_general(
                target_ref[...] * gvalue, onehot, LANE_DIMS, precision=HIGHEST,
                preferred_element_type=jnp.float32,
            )
            for copy in term_copies:
                copy.start()

    for copy in term_copies:
        copy.wait_recv()
    total = terms[0]
    for d in range(1, n_rows):
        total = total + terms[d]
    share = classes // n_rows
    pick = (
        lax.broadcasted_iota(jnp.int32, (classes, share), 0)
        == lax.broadcasted_iota(jnp.int32, (classes, share), 1) + me * share
    ).astype(jnp.float32)
    grad_ref[...] = jnp.dot(
        total, pick, precision=HIGHEST, preferred_element_type=jnp.float32
    )[:1]

    for peers, to_mate, to_near, forwards in started:
        for copy in peers + [to_mate] + to_near + forwards:
            copy.wait_send()
    for copy in term_copies:
        copy.wait_send()


def on_device(n_rows, n_patch, panel, pairing, hop_blocks, hop_cols, bnd_weight, attract, attract_class, target):
    _, rows, width = panel.shape
    edge = bnd_weight.shape[0]
    classes = attract.shape[0]
    n_chunks = 2 * (width // LANES)
    n_near = len(distinct(n_patch))
    n_peers = n_rows // 2 - 1
    dma = pltpu.SemaphoreType.DMA
    vmem = pl.BlockSpec(memory_space=pltpu.VMEM)
    in_hbm = pl.BlockSpec(memory_space=pltpu.HBM)

    blocks = rows // BLOCK

    def each(count):
        return [pltpu.VMEM((count, BLOCK, LANES), jnp.bfloat16) for _ in range(n_chunks)]

    cheb_two, new_pair, class_grad = pl.pallas_call(
        functools.partial(kernel, n_rows, n_patch),
        out_shape=(
            pltpu.VMEM((2, blocks, BLOCK, width), jnp.bfloat16),
            pltpu.VMEM((1, rows), jnp.float32),
            pltpu.VMEM((1, classes // n_rows), jnp.float32),
        ),
        in_specs=[pl.BlockSpec(memory_space=pltpu.SMEM)] + [vmem, in_hbm] + [vmem] * 3 + [in_hbm] * 2,
        out_specs=(vmem, vmem, vmem),
        scratch_shapes=[
            each(n_rows * blocks),
            each(n_rows * blocks),
            each(n_near * edge // BLOCK),
            each(n_near * edge // BLOCK),
            pltpu.VMEM(hop_blocks.shape, jnp.bfloat16),
            pltpu.VMEM((rows, LANES), jnp.float32),
            pltpu.VMEM((rows, LANES), jnp.float32),
            pltpu.VMEM((n_rows, 8, classes), jnp.float32),
            dma((2 * n_chunks, n_peers)),
            dma((2 * n_chunks, n_peers)),
            dma((2 * n_chunks,)),
            dma((2 * n_chunks,)),
            dma((2 * n_chunks, n_peers)),
            dma((2 * n_chunks, n_peers)),
            dma((2 * n_chunks, n_near)),
            dma((2 * n_chunks, n_near)),
            dma((n_rows - 1,)),
            dma((n_rows - 1,)),
            dma((n_chunks,)),
            dma,
            pltpu.VMEM(bnd_weight.shape, jnp.bfloat16),
            dma,
        ],
        compiler_params=pltpu.CompilerParams(
            collective_id=0, has_side_effects=True, vmem_limit_bytes=56 * 1024 * 1024
        ),
    )(
        hop_cols, pairing.reshape(1, rows), bnd_weight, attract.reshape(1, classes),
        attract_class.reshape(1, rows), target.reshape(1, rows),
        panel.reshape(2, blocks, BLOCK, width), hop_blocks,
    )
    return cheb_two.reshape(panel.shape), new_pair.reshape(rows), class_grad


def solution(mesh):
    return jax.shard_map(
        functools.partial(on_device, mesh.shape["rows"], mesh.shape["patch"]),
        mesh=mesh,
        in_specs=(
            P(None, ("groups", "patch", "rows"), None),
            P(("groups", "patch", "rows")),
            P(("groups", "patch", "rows"), None, None, None),
            P(("groups", "patch", "rows"), None),
            P(("groups", "patch", "rows"), None),
            P(),
            P(("groups", "patch", "rows")),
            P(("groups", "patch", "rows")),
        ),
        out_specs=(
            P(None, ("groups", "patch", "rows"), None),
            P(("groups", "patch", "rows")),
            P(("groups", "patch"), "rows"),
        ),
        check_vma=False,
    )
```

```python
import functools

import jax
import jax.numpy as jnp
from jax import lax
from jax.experimental import pallas as pl
from jax.experimental.pallas import tpu as pltpu
from jax.sharding import PartitionSpec as P

coef_zero = 0.5
coef_one = 0.55
coef_two = -0.3

LANES = 128
BLOCK = 128
OFFSETS = (-1, 1, -2, 2)
MESH = pl.DeviceIdType.MESH
HIGHEST = lax.Precision.HIGHEST
LANE_DIMS = (((1,), (1,)), ((), ()))


def distinct(n_patch):
    shifts = []
    for offset in OFFSETS:
        if offset % n_patch not in shifts:
            shifts.append(offset % n_patch)
    return shifts


def kernel(
    n_rows, n_patch,
    cols_ref, pairing_ref, bnd_hbm, attract_ref, class_ref, target_ref, panel_ref, hop_ref,
    cheb_ref, small_ref,
    pbufs, fbufs, pnear, fnear, hop, pair, moments, terms,
    peer_send, peer_recv, mate_send, mate_recv, fwd_send, fwd_recv,
    near_send, near_recv, term_send, term_recv, load_sem, hop_sem, bnd_ref, bnd_sem,
):
    n_blocks = panel_ref.shape[1]
    rows = n_blocks * BLOCK
    width = panel_ref.shape[3]
    edge = bnd_ref.shape[0]
    edge_blocks = edge // BLOCK
    classes = attract_ref.shape[1]
    n_links = hop_ref.shape[1]
    halves = width // LANES
    shifts = distinct(n_patch)
    chunks = [(c, k) for c in range(2) for k in range(halves)]
    n_chunks = len(chunks)
    n_peers = n_rows // 2 - 1

    me = lax.axis_index("rows")
    patch = lax.axis_index("patch")
    mate = me + 1 - 2 * lax.rem(me, 2)

    def row_id(distance):
        return lax.rem(me + distance, n_rows)

    def span(owner):
        return pl.ds(owner * n_blocks, n_blocks)

    def patch_id(shift):
        return lax.rem(patch + shift, n_patch)

    barrier = pltpu.get_barrier_semaphore()
    for shift in reversed(shifts):
        pl.semaphore_signal(barrier, inc=1, device_id={"patch": patch_id(shift)}, device_id_type=MESH)
    for distance in range(1, n_rows):
        pl.semaphore_signal(barrier, inc=1, device_id={"rows": row_id(distance)}, device_id_type=MESH)

    bnd_copy = pltpu.make_async_copy(bnd_hbm, bnd_ref, bnd_sem)
    hop_copy = pltpu.make_async_copy(hop_ref, hop, hop_sem)
    loads = []
    for i, (c, k) in enumerate(chunks):
        lanes = pl.ds(k * LANES, LANES)
        loads.append(
            pltpu.make_async_copy(panel_ref.at[c, :, :, lanes], pbufs[i].at[span(me)], load_sem.at[i])
        )
        loads[i].start()
    hop_copy.start()
    bnd_copy.start()
    pl.semaphore_wait(barrier, n_rows - 1 + len(shifts))

    def sends(step, own, slab, dest, near):
        peers = [
            pltpu.make_async_remote_copy(
                own, dest.at[span(me)], peer_send.at[step, j], peer_recv.at[step, j],
                device_id={"rows": row_id(n_rows - 2 * (j + 1))}, device_id_type=MESH,
            )
            for j in range(n_peers)
        ]
        to_mate = pltpu.make_async_remote_copy(
            own, dest.at[span(me)], mate_send.at[step], mate_recv.at[step],
            device_id={"rows": mate}, device_id_type=MESH,
        )
        to_near = [
            pltpu.make_async_remote_copy(
                slab, near.at[pl.ds(j * edge_blocks, edge_blocks)], near_send.at[step, j], near_recv.at[step, j],
                device_id={"patch": patch_id(n_patch - shift)}, device_id_type=MESH,
            )
            for j, shift in enumerate(shifts)
        ]
        forwards = []
        for j in range(n_peers):
            block = dest.at[span(row_id(2 * (j + 1)))]
            forwards.append(
                pltpu.make_async_remote_copy(
                    block, block, fwd_send.at[step, j], fwd_recv.at[step, j],
                    device_id={"rows": mate}, device_id_type=MESH,
                )
            )
        return peers, to_mate, to_near, forwards

    def launch(copies):
        peers, to_mate, to_near, _ = copies
        for copy in peers + to_near + [to_mate]:
            copy.start()

    def arrive(copies):
        peers, to_mate, to_near, forwards = copies
        for peer, forward in zip(peers, forwards):
            peer.wait_recv()
            forward.start()
        to_mate.wait_recv()
        for copy in to_near:
            copy.wait_recv()
        for forward in forwards:
            forward.wait_recv()

    def hopped(buf, near, b):
        left = [hop[b, n] for n in range(n_links)]
        right = [buf[cols_ref[b, n]] for n in range(n_links)]
        if b * BLOCK < edge:
            left.append(bnd_ref[pl.ds(b * BLOCK, BLOCK), :])
            for offset in OFFSETS:
                slot = shifts.index(offset % n_patch) * edge_blocks
                right.extend(near[slot + e] for e in range(edge_blocks))
        return jnp.dot(
            jnp.concatenate(left, axis=1),
            jnp.concatenate(right, axis=0),
            preferred_element_type=jnp.float32,
        )

    started = []
    for i, (c, k) in enumerate(chunks):
        lanes = pl.ds(k * LANES, LANES)
        started.append(
            sends(i, panel_ref.at[c, :, :, lanes], panel_ref.at[c, pl.ds(0, edge_blocks), :, lanes], pbufs[i], pnear[i])
        )
        for copy in started[i][0]:
            copy.start()
    for _, to_mate, to_near, _ in started:
        for copy in to_near + [to_mate]:
            copy.start()

    for b in range(rows // BLOCK):
        sites = pl.ds(b * BLOCK, BLOCK)
        wide = jnp.broadcast_to(pairing_ref[:, sites], (BLOCK, BLOCK))
        pair[sites, :] = wide.T

    hop_copy.wait()
    bnd_copy.wait()
    for i in range(n_chunks):
        loads[i].wait()

    for i, (c, k) in enumerate(chunks):
        arrive(started[i])
        other = (1 - c) * halves + k
        for b in range(rows // BLOCK):
            sites = pl.ds(b * BLOCK, BLOCK)
            hv = hopped(pbufs[i], pnear[i], b)
            cross = pair[sites, :] * pbufs[other][me * n_blocks + b].astype(jnp.float32)
            value = cross + hv if c == 0 else cross - hv
            fbufs[i][me * n_blocks + b] = value.astype(jnp.bfloat16)
        started.append(
            sends(
                n_chunks + i, fbufs[i].at[span(me)],
                fbufs[i].at[pl.ds(me * n_blocks, edge_blocks)], fbufs[i], fnear[i],
            )
        )
        launch(started[n_chunks + i])

    term_copies = [
        pltpu.make_async_remote_copy(
            terms.at[0], terms.at[d], term_send.at[d - 1], term_recv.at[d - 1],
            device_id={"rows": row_id(n_rows - d)}, device_id_type=MESH,
        )
        for d in range(1, n_rows)
    ]
    def add_terms():
        for copy in term_copies:
            copy.wait_recv()
        total = terms[0]
        for d in range(1, n_rows):
            total = total + terms[d]
        share = classes // n_rows
        pick = (
            lax.broadcasted_iota(jnp.int32, (classes, share), 0)
            == lax.broadcasted_iota(jnp.int32, (classes, share), 1) + me * share
        ).astype(jnp.float32)
        small_ref[:, pl.ds(rows, share)] = jnp.dot(
            total, pick, precision=HIGHEST, preferred_element_type=jnp.float32
        )[:1]

    for i, (c, k) in enumerate(chunks):
        if i == n_chunks - 1:
            add_terms()
        arrive(started[n_chunks + i])
        other = (1 - c) * halves + k
        for b in range(rows // BLOCK):
            sites = pl.ds(b * BLOCK, BLOCK)
            mine = me * n_blocks + b
            hv = hopped(fbufs[i], fnear[i], b)
            cross = pair[sites, :] * fbufs[other][mine].astype(jnp.float32)
            before = pbufs[i][mine].astype(jnp.float32)
            second = 2.0 * (cross + hv if c == 0 else cross - hv) - before
            cheb_ref[c, b, :, pl.ds(k * LANES, LANES)] = second.astype(jnp.bfloat16)
            if c == 0:
                moment = (
                    coef_zero * before
                    + coef_one * fbufs[i][mine].astype(jnp.float32)
                    + coef_two * second
                )
                weighted = pbufs[other][mine].astype(jnp.float32) * moment
                if k == 0:
                    moments[sites, :] = weighted
                else:
                    moments[sites, :] += weighted
        if c == 0 and k == halves - 1:
            ones = jnp.ones((8, LANES), jnp.float32)
            gvalue = lax.dot_general(
                ones, moments[...], LANE_DIMS, precision=HIGHEST,
                preferred_element_type=jnp.float32,
            ) / width
            numbers = lax.broadcasted_iota(jnp.int32, (classes, rows), 0)
            onehot = (numbers == class_ref[...]).astype(jnp.float32)
            gain = jnp.dot(
                jnp.broadcast_to(attract_ref[...], (8, classes)), onehot, precision=HIGHEST,
                preferred_element_type=jnp.float32,
            )
            small_ref[:, pl.ds(0, rows)] = (gain * gvalue)[:1]
            terms[0] = lax.dot_general(
                target_ref[...] * gvalue, onehot, LANE_DIMS, precision=HIGHEST,
                preferred_element_type=jnp.float32,
            )
            for copy in term_copies:
                copy.start()

    for peers, to_mate, to_near, forwards in started:
        for copy in peers + [to_mate] + to_near + forwards:
            copy.wait_send()
    for copy in term_copies:
        copy.wait_send()


def on_device(n_rows, n_patch, panel, pairing, hop_blocks, hop_cols, bnd_weight, attract, attract_class, target):
    _, rows, width = panel.shape
    edge = bnd_weight.shape[0]
    classes = attract.shape[0]
    n_chunks = 2 * (width // LANES)
    n_near = len(distinct(n_patch))
    n_peers = n_rows // 2 - 1
    dma = pltpu.SemaphoreType.DMA
    vmem = pl.BlockSpec(memory_space=pltpu.VMEM)
    in_hbm = pl.BlockSpec(memory_space=pltpu.HBM)

    blocks = rows // BLOCK

    def each(count):
        return [pltpu.VMEM((count, BLOCK, LANES), jnp.bfloat16) for _ in range(n_chunks)]

    cheb_two, small = pl.pallas_call(
        functools.partial(kernel, n_rows, n_patch),
        out_shape=(
            pltpu.VMEM((2, blocks, BLOCK, width), jnp.bfloat16),
            pltpu.VMEM((1, rows + classes // n_rows), jnp.float32),
        ),
        in_specs=[pl.BlockSpec(memory_space=pltpu.SMEM)] + [vmem, in_hbm] + [vmem] * 3 + [in_hbm] * 2,
        out_specs=(vmem, vmem),
        scratch_shapes=[
            each(n_rows * blocks),
            each(n_rows * blocks),
            each(n_near * edge // BLOCK),
            each(n_near * edge // BLOCK),
            pltpu.VMEM(hop_blocks.shape, jnp.bfloat16),
            pltpu.VMEM((rows, LANES), jnp.float32),
            pltpu.VMEM((rows, LANES), jnp.float32),
            pltpu.VMEM((n_rows, 8, classes), jnp.float32),
            dma((2 * n_chunks, n_peers)),
            dma((2 * n_chunks, n_peers)),
            dma((2 * n_chunks,)),
            dma((2 * n_chunks,)),
            dma((2 * n_chunks, n_peers)),
            dma((2 * n_chunks, n_peers)),
            dma((2 * n_chunks, n_near)),
            dma((2 * n_chunks, n_near)),
            dma((n_rows - 1,)),
            dma((n_rows - 1,)),
            dma((n_chunks,)),
            dma,
            pltpu.VMEM(bnd_weight.shape, jnp.bfloat16),
            dma,
        ],
        compiler_params=pltpu.CompilerParams(
            collective_id=0, has_side_effects=True, vmem_limit_bytes=56 * 1024 * 1024
        ),
    )(
        hop_cols, pairing.reshape(1, rows), bnd_weight, attract.reshape(1, classes),
        attract_class.reshape(1, rows), target.reshape(1, rows),
        panel.reshape(2, blocks, BLOCK, width), hop_blocks,
    )
    return cheb_two.reshape(panel.shape), small[0, :rows], small[:, rows:]


def solution(mesh):
    return jax.shard_map(
        functools.partial(on_device, mesh.shape["rows"], mesh.shape["patch"]),
        mesh=mesh,
        in_specs=(
            P(None, ("groups", "patch", "rows"), None),
            P(("groups", "patch", "rows")),
            P(("groups", "patch", "rows"), None, None, None),
            P(("groups", "patch", "rows"), None),
            P(("groups", "patch", "rows"), None),
            P(),
            P(("groups", "patch", "rows")),
            P(("groups", "patch", "rows")),
        ),
        out_specs=(
            P(None, ("groups", "patch", "rows"), None),
            P(("groups", "patch", "rows")),
            P(("groups", "patch"), "rows"),
        ),
        check_vma=False,
    )
```
